32 devices in a mesh: freq: 2 (over y), src: 4 (over z), tgt: 2 (over x), pol: 2 (over core).
Axes of the slice: x: 2, y: 2, z: 4, core: 2. Of those that a mesh axis runs over, the one named last changes fastest.
Arguments:
- sub_points: float32 [3, 4096], P(None, 'src'), may hold values from -1 to 1
- sub_currents: bfloat16 [2, 4096, 128], P('pol', 'src'), may hold values from -6 to 6
- main_points: float32 [3, 1024], P(None, ('src', 'tgt')), may hold values from 2 to 6
- main_weight: float32 [1024], P(('src', 'tgt')), may hold values from 0.3 to 3
- panel_ids: int32 [1024], P(('src', 'tgt')), may hold values from 0 to 63
- panel_shift: float32 [64], replicated, may hold values from -0.05 to 0.05
- theta: float32 [128], replicated, may hold values from 0 to 0.6
- phi: float32 [128], replicated, may hold values from -3.140625 to 3.140625
- wavenumber: float32 [2], P('freq'), parts along dimension 0, may hold values from 20 to 60
Outputs:
- main_current: bfloat16 [2, 1024, 256], P('pol', ('src', 'tgt'), 'freq'), parts along dimension 2
- far_field: float32 [2, 128, 256], P('pol', ('src', 'tgt'), 'freq'), parts along dimension 2
The draws below stay inside these ranges and needn't reach their ends.
There are 2 independent parts, one for each index of `freq`. The reference program is written for one: setup_inputs(seed, part) draws one part's arguments, and reference() takes and returns one part's arrays. A program takes and returns all parts, laid end to end along the dimension named above; an argument that names none is the same for every part. Nothing has to cross between parts.
All inputs are finite; a program needn't handle non-finite values.
Results may differ from the reference program's by a relative error of at most 0.0056.
Values may be sent and summed in bfloat16 or wider, within the bound.
A program may use at most 64 MiB of HBM per device.

```python
import math
import jax
import jax.numpy as jnp
from jax import lax

BEAMS = 64
PANELS = 64
SUB = 4096
MAIN = 1024
DIR = 128


def touch_ends(entries, stream_key, smallest, high):
    shape = entries.shape
    spot = [jax.random.randint(jax.random.fold_in(stream_key, axis), (), 0, shape[axis]) for axis in range(len(shape))]
    entries = entries.at[tuple(spot)].set(smallest)
    longest = shape.index(max(shape))
    spot[longest] = (spot[longest] + 1) % shape[longest]
    return entries.at[tuple(spot)].set(high)


def shard_levels(own_key, shape, cuts, low, top_value):
    def one(dim, parts):
        steps = jax.random.uniform(jax.random.fold_in(jax.random.fold_in(own_key, 6), dim), (parts,), jnp.float32, low / len(cuts), top_value / len(cuts))
        return jnp.repeat(jnp.exp(steps), shape[dim] // parts).reshape((-1,) + (1,) * (len(shape) - dim - 1))

    gain = one(*cuts[0])
    for cut in cuts[1:]:
        gain = gain * one(*cut)
    return gain


def normal_values(stream_key, dims, deviation, bound, cuts=(), dtype=jnp.bfloat16):
    drawn = jax.random.normal(stream_key, dims, jnp.float32) * deviation
    if len(cuts) > 0:
        drawn = shard_levels(stream_key, dims, cuts, -0.22, 0.18) * drawn
    return jnp.clip(drawn, min=-bound, max=bound).astype(dtype)


def setup_inputs(seed: int = 0, part: int = 0) -> dict:
    key_of = jax.random.split(jax.random.key(seed), 10)
    part_splits = jax.random.split(jax.random.fold_in(key_of[9], part), 10)
    sub_points = jnp.clip(jax.random.uniform(key_of[0], (3, SUB), jnp.float32, -1.0, 1.0) * shard_levels(key_of[0], (3, SUB), ((1, 4),), -0.4, 0.0), -1.0, 1.0)
    sub_currents = normal_values(key_of[1], (2, SUB, 2 * BEAMS), 1.0, 6.0, ((0, 2), (1, 4)))
    main_points = jnp.clip(2.0 + 4.0 * jax.random.uniform(key_of[2], (3, MAIN), jnp.float32) ** shard_levels(key_of[2], (3, MAIN), ((1, 8),), -0.2, 0.2), 2.0, 6.0)
    main_weight = jnp.clip(jnp.exp(math.log(3.0) - 2.3025851 * jax.random.uniform(key_of[3], (MAIN,), jnp.float32) ** shard_levels(key_of[3], (MAIN,), ((0, 8),), -0.2, 0.2)), 0.3, 3.0)
    panel_ids = touch_ends(jax.random.randint(key_of[4], (MAIN,), 0, PANELS), jax.random.fold_in(key_of[4], 1), 0, PANELS - 1).astype(jnp.int32)
    panel_shift = jnp.clip(jax.random.uniform(key_of[5], (PANELS,), jnp.float32, -0.05, 0.05), -0.05, 0.05)
    theta = jnp.clip(jax.random.uniform(key_of[6], (DIR,), jnp.float32, 0.0, 0.6), 0.0, 0.6)
    phi = jnp.clip(jax.random.uniform(key_of[7], (DIR,), jnp.float32, -3.140625, 3.140625), -3.140625, 3.140625)
    wavenumber = jnp.clip(jnp.exp(jax.random.uniform(part_splits[8], (1,), jnp.float32, math.log(20.0), math.log(60.0))), 20.0, 60.0)
    return {"sub_points": sub_points, "sub_currents": sub_currents, "main_points": main_points, "main_weight": main_weight, "panel_ids": panel_ids, "panel_shift": panel_shift, "theta": theta, "phi": phi, "wavenumber": wavenumber}


def blockwise(worker, points):
    total_rows = points.shape[1]
    block_rows = 512
    if total_rows > block_rows and total_rows % block_rows == 0:
        blocks = points.reshape(3, total_rows // block_rows, block_rows).transpose(1, 0, 2)
        result = lax.map(worker, blocks)
        return result.reshape(total_rows, result.shape[-1])
    return worker(points)

def rotated(current):
    half_cols = current.shape[1] // 2
    lower = jnp.concatenate([-current[:, half_cols:], current[:, :half_cols]], 1)
    return jnp.concatenate([current, lower], 0)

def near_kernel(targets, sources, wave_number):
    differ = targets[0][:, None] - sources[0][None, :]
    square = differ * differ
    differ = targets[1][:, None] - sources[1][None, :]
    square = square + differ * differ
    differ = targets[2][:, None] - sources[2][None, :]
    square = square + differ * differ
    radius = jnp.sqrt(square)
    phase = wave_number * radius
    real_part = (4.0 * jnp.cos(phase) / radius).astype(jnp.bfloat16)
    imag_part = (-4.0 * jnp.sin(phase) / radius).astype(jnp.bfloat16)
    return jnp.concatenate([real_part, imag_part], 1)

def far_kernel(unit_dirs, sources, wave_number):
    inner = unit_dirs[0][:, None] * sources[0][None, :] + unit_dirs[1][:, None] * sources[1][None, :]
    inner = inner + unit_dirs[2][:, None] * sources[2][None, :]
    phase = wave_number * inner
    real_part = jnp.cos(phase).astype(jnp.bfloat16)
    imag_part = jnp.sin(phase).astype(jnp.bfloat16)
    return jnp.concatenate([real_part, imag_part], 1)

def currents_from(induced, weight, angle):
    half_cols = induced.shape[1] // 2
    real_in = induced[:, :half_cols]
    imag_in = induced[:, half_cols:]
    cosine = jnp.cos(angle)[:, None]
    sine = jnp.sin(angle)[:, None]
    real_out = weight[:, None] * (real_in * cosine + imag_in * sine)
    imag_out = weight[:, None] * (imag_in * cosine - real_in * sine)
    return jnp.concatenate([real_out, imag_out], 1).astype(jnp.bfloat16)

def directions(theta, phi):
    return jnp.stack([jnp.sin(theta) * jnp.cos(phi), jnp.sin(theta) * jnp.sin(phi), jnp.cos(theta)], 0)

def reference(sub_points, sub_currents, main_points, main_weight, panel_ids, panel_shift, theta, phi, wavenumber):
    wave_number = wavenumber[0]
    columns = sub_currents.shape[2]
    near_weights = jnp.concatenate([rotated(sub_currents[0]), rotated(sub_currents[1])], 1)

    def first_section(points_block):
        return jnp.dot(near_kernel(points_block, sub_points, wave_number), near_weights, preferred_element_type=jnp.float32)
    induced = blockwise(first_section, main_points) * (1.0 / math.sqrt(SUB))
    angle = 2.0 * wave_number * panel_shift[panel_ids]
    current_x = currents_from(induced[:, :columns], main_weight, angle)
    current_y = currents_from(induced[:, columns:], main_weight, angle)
    far_weights = jnp.concatenate([rotated(current_x), rotated(current_y)], 1)

    def second_section(points_block):
        return jnp.dot(far_kernel(points_block, main_points, wave_number), far_weights, preferred_element_type=jnp.float32)
    radiated = blockwise(second_section, directions(theta, phi)) * (1.0 / math.sqrt(MAIN))
    field_x = radiated[:, :columns]
    field_y = radiated[:, columns:]
    cos_phi = jnp.cos(phi)[:, None]
    sin_phi = jnp.sin(phi)[:, None]
    co_polar = cos_phi * field_x + sin_phi * field_y
    cross_polar = cos_phi * field_y - sin_phi * field_x
    return (jnp.stack([current_x, current_y], 0), jnp.stack([co_polar, cross_polar], 0))
```

```python
import functools
import math

import jax
import jax.numpy as jnp
from jax import lax
from jax.experimental import pallas as pl
from jax.experimental.pallas import tpu as pltpu
from jax.sharding import PartitionSpec as P

MESH = pl.DeviceIdType.MESH
TURN = 2.0 * math.pi
COS_HALF = (1.4142135381698608, -6.978850841522217, 5.739460468292236, -1.8835580348968506, 0.3106880187988281)
SIN_HALF = (4.442879676818848, -7.307816505432129, 3.5977745056152344, -0.7911993861198425)


def poly(coefs, s):
    value = coefs[-1]
    for coef in coefs[-2::-1]:
        value = value * s + coef
    return value


def turn_cos_sin(t):
    f = t - jnp.round(t)
    s = f * f
    half_cos = poly(COS_HALF, s)
    half_sin = f * poly(SIN_HALF, s)
    return 1.0 - half_sin * half_sin, half_cos * half_sin


def each(count, body, start=0):
    if count <= 16:
        for i in range(start, count):
            body(i)
    else:
        lax.fori_loop(start, count, lambda i, c: (body(i), c)[1], 0)


def thirds(x):
    first = x.astype(jnp.bfloat16).astype(jnp.float32)
    rest = x - first
    second = rest.astype(jnp.bfloat16).astype(jnp.float32)
    return first, second, rest - second


def left_rows(x):
    a, b, c = thirds(x)
    return jnp.concatenate([a, a, b, b, a, c], 0)


def right_rows(x):
    a, b, c = thirds(x)
    return jnp.concatenate([a, b, a, b, c, a], 0).astype(jnp.bfloat16)


def stack_rows(rows):
    n = rows[0].shape[1]
    index = lax.broadcasted_iota(jnp.int32, (8, n), 0)
    out = jnp.zeros((8, n), jnp.float32)
    for i, row in enumerate(rows):
        out = jnp.where(index == i, row, out)
    return out


def columns(rows):
    return jnp.transpose(stack_rows(rows))


def inner(left, right):
    lhs = jnp.transpose(left_rows(left)).astype(jnp.bfloat16)
    return jnp.dot(lhs, right_rows(right), preferred_element_type=jnp.float32)


def swapped(x):
    return pltpu.roll(x, x.shape[1] // 2, 1)


def kernel(
    S, T, sub_total, main_total,
    wave, sub_pts, sub_cur, main_pts, weight, ids, shift, theta, phi,
    cur_out, far_out,
    v_sub, v_cur, v_pts, v_weight, v_ids, v_shift, v_theta, v_phi,
    r2, kern, fkern, part, part_in, rad_own, rad_out, rad_in, phi_cols, cur_cols,
    in_sem, a_send, a_recv, b_send, b_recv, c_send, c_recv,
):
    rows = main_pts.shape[1]
    subs = sub_pts.shape[1]
    dirs = theta.shape[1]
    cols = sub_cur.shape[2]
    src, tgt, pol = lax.axis_index("src"), lax.axis_index("tgt"), lax.axis_index("pol")
    N = S * T * 2
    own_rows = dirs // (S * T)
    flat = (src * T + tgt) * 2 + pol

    def member(d):
        other = lax.rem(flat + d, N)
        return other, {"src": other // (T * 2), "tgt": lax.rem(other // 2, T), "pol": lax.rem(other, 2)}

    barrier = pltpu.get_barrier_semaphore()

    def greet(d):
        pl.semaphore_signal(barrier, inc=1, device_id=member(d)[1], device_id_type=MESH)

    each(N, greet, 1)

    loads = [
        pltpu.make_async_copy(a, b, in_sem.at[i])
        for i, (a, b) in enumerate([
            (main_pts, v_pts.at[0]), (sub_pts, v_sub), (theta, v_theta), (phi, v_phi),
            (weight, v_weight), (ids, v_ids), (shift, v_shift), (sub_cur.at[0], v_cur),
        ])
    ]
    for load in loads:
        load.start()
    pl.semaphore_wait(barrier, N - 1)

    def to_owner(d):
        return {"src": lax.rem(src + S - d, S)}

    def send_points(d):
        pltpu.make_async_remote_copy(
            main_pts, v_pts.at[d], a_send.at[d], a_recv.at[d],
            device_id={"src": lax.rem(src + d, S)}, device_id_type=MESH,
        ).start()

    each(S, send_points, 1)

    q = wave[0] * (1.0 / TURN)
    low_half = lax.broadcasted_iota(jnp.int32, (1, cols), 1) < cols // 2
    sign = jnp.where(low_half, 1.0, -1.0)

    for load in loads[:2]:
        load.wait()
    sx, sy, sz = (v_sub[i : i + 1, :] * q for i in range(3))
    one = jnp.ones_like(sx)
    sub_side = right_rows(stack_rows([sx, sy, sz, one, sx * sx + sy * sy + sz * sz]))

    def near_block(d, slot):
        x, y, z = (v_pts[d, i : i + 1, :] * q for i in range(3))
        main_side = stack_rows(
            [-2.0 * x, -2.0 * y, -2.0 * z, x * x + y * y + z * z, jnp.ones_like(x)]
        )
        r2[slot] = inner_with(main_side, sub_side)
        step = 16
        for at in range(0, rows, step):
            square = r2[slot, at : at + step, :]
            inverse = lax.rsqrt(square)
            cosine, sine = turn_cos_sin(square * inverse)
            kern[slot, at : at + step, :] = (cosine * inverse).astype(jnp.bfloat16)
            kern[slot, rows + at : rows + at + step, :] = (sine * inverse).astype(jnp.bfloat16)
        both = jnp.dot(kern[slot], v_cur[...], preferred_element_type=jnp.float32)
        return both[:rows] + sign * swapped(both[rows:])

    def inner_with(left, right):
        lhs = jnp.transpose(left_rows(left)).astype(jnp.bfloat16)
        return jnp.dot(lhs, right, preferred_element_type=jnp.float32)

    for load in loads[2:]:
        load.wait()
    cos_t, sin_t = turn_cos_sin(v_theta[...] * (1.0 / TURN))
    cos_p, sin_p = turn_cos_sin(v_phi[...] * (1.0 / TURN))
    phi_cols[...] = columns([cos_p, sin_p])
    units = stack_rows([sin_t * cos_p, sin_t * sin_p, cos_t])
    px, py, pz = (v_pts[0, i : i + 1, :] * q for i in range(3))
    unit_side = jnp.transpose(left_rows(units)).astype(jnp.bfloat16)
    turns = jnp.dot(
        unit_side, right_rows(stack_rows([px, py, pz])), preferred_element_type=jnp.float32
    )
    step = 128
    for at in range(0, dirs, step):
        cosine, sine = turn_cos_sin(turns[at : at + step])
        fkern[at : at + step, :] = cosine.astype(jnp.bfloat16)
        fkern[dirs + at : dirs + at + step, :] = sine.astype(jnp.bfloat16)

    cols_in = columns([v_weight[...], v_ids[...].astype(jnp.float32)])
    panel = lax.broadcasted_iota(jnp.int32, (rows, shift.shape[1]), 1).astype(jnp.float32)
    chosen = jnp.sum(jnp.where(cols_in[:, 1:2] == panel, v_shift[...], 0.0), 1, keepdims=True)
    cos_a, sin_a = turn_cos_sin(jnp.broadcast_to(2.0 * q * chosen, (rows, cols)))
    scale = 4.0 * q * (1.0 / math.sqrt(sub_total))
    factor = scale * cols_in[:, 0:1]
    cur_cols[0] = factor * cos_a
    cur_cols[1] = factor * sin_a * sign

    own = near_block(0, 0)

    def remote_block(d):
        pltpu.make_async_remote_copy(
            main_pts, v_pts.at[d], a_send.at[d], a_recv.at[d],
            device_id=to_owner(d), device_id_type=MESH,
        ).wait()
        part[d] = near_block(d, d % 2).astype(jnp.bfloat16)
        pltpu.make_async_remote_copy(
            part.at[d], part_in.at[d], b_send.at[d], b_recv.at[d],
            device_id=to_owner(d), device_id_type=MESH,
        ).start()

    each(S, remote_block, 1)

    def landed(d):
        pltpu.make_async_remote_copy(
            part.at[d], part_in.at[d], b_send.at[d], b_recv.at[d],
            device_id=to_owner(d), device_id_type=MESH,
        ).wait()

    each(S, landed, 1)
    induced = own
    if S <= 16:
        for d in range(1, S):
            induced = induced + part_in[d].astype(jnp.float32)
    else:
        induced = lax.fori_loop(
            1, S, lambda d, total: total + part_in[d].astype(jnp.float32), induced
        )
    current = (induced * cur_cols[0] + swapped(induced) * cur_cols[1]).astype(jnp.bfloat16)
    cur_out[0] = current

    for at in range(0, dirs, step):
        real = jnp.dot(fkern[at : at + step], current, preferred_element_type=jnp.float32)
        imag = jnp.dot(
            fkern[dirs + at : dirs + at + step], current, preferred_element_type=jnp.float32
        )
        field = real - sign * swapped(imag)
        rad_own[at : at + step] = field
        rad_out[at : at + step] = field.astype(jnp.bfloat16)

    def far_copy(d):
        other, where = member(d)
        first = pl.multiple_of(other // 2 * own_rows, own_rows)
        return pltpu.make_async_remote_copy(
            rad_out.at[pl.ds(first, own_rows)], rad_in.at[d], c_send.at[d], c_recv.at[d],
            device_id=where, device_id_type=MESH,
        )

    each(N, lambda d: far_copy(d).start(), 1)
    each(N, lambda d: far_copy(d).wait(), 1)

    here = pl.ds(pl.multiple_of((src * T + tgt) * own_rows, own_rows), own_rows)
    mine = rad_own[here]
    theirs = rad_in[1].astype(jnp.float32)

    def gathered(d, pair):
        return (
            pair[0] + rad_in[2 * d].astype(jnp.float32),
            pair[1] + rad_in[2 * d + 1].astype(jnp.float32),
        )

    if N <= 16:
        for d in range(1, N // 2):
            mine, theirs = gathered(d, (mine, theirs))
    else:
        mine, theirs = lax.fori_loop(1, N // 2, gathered, (mine, theirs))
    angles = phi_cols[here]
    flip = 1.0 - 2.0 * pol.astype(jnp.float32)
    far_out[0] = (angles[:, 0:1] * mine + (flip * angles[:, 1:2]) * theirs) * (
        1.0 / math.sqrt(main_total)
    )


def on_device(S, T, sub_points, sub_currents, main_points, main_weight, panel_ids, panel_shift, theta, phi, wavenumber):
    rows, subs = main_points.shape[1], sub_points.shape[1]
    cols = sub_currents.shape[2]
    dirs = theta.shape[0]
    panels = panel_shift.shape[0]
    N = S * T * 2
    own_rows = dirs // (S * T)
    f32, bf16 = jnp.float32, jnp.bfloat16
    hbm = pl.BlockSpec(memory_space=pl.ANY)
    vmem = pl.BlockSpec(memory_space=pltpu.VMEM)
    dma = pltpu.SemaphoreType.DMA
    return pl.pallas_call(
        functools.partial(kernel, S, T, subs * S, rows * S * T),
        out_shape=(
            jax.ShapeDtypeStruct((1, rows, cols), bf16),
            jax.ShapeDtypeStruct((1, own_rows, cols), f32),
        ),
        in_specs=[pl.BlockSpec(memory_space=pltpu.SMEM)] + [hbm] * 8,
        out_specs=(vmem, vmem),
        scratch_shapes=[
            pltpu.VMEM((3, subs), f32),
            pltpu.VMEM((subs, cols), bf16),
            pltpu.VMEM((S, 3, rows), f32),
            pltpu.VMEM((1, rows), f32),
            pltpu.VMEM((1, rows), jnp.int32),
            pltpu.VMEM((1, panels), f32),
            pltpu.VMEM((1, dirs), f32),
            pltpu.VMEM((1, dirs), f32),
            pltpu.VMEM((2, rows, subs), f32),
            pltpu.VMEM((2, 2 * rows, subs), bf16),
            pltpu.VMEM((2 * dirs, rows), bf16),
            pltpu.VMEM((S, rows, cols), bf16),
            pltpu.VMEM((S, rows, cols), bf16),
            pltpu.VMEM((dirs, cols), f32),
            pltpu.VMEM((dirs, cols), bf16),
            pltpu.VMEM((N, own_rows, cols), bf16),
            pltpu.VMEM((dirs, 8), f32),
            pltpu.VMEM((2, rows, cols), f32),
            dma((8,)),
            dma((S,)),
            dma((S,)),
            dma((S,)),
            dma((S,)),
            dma((N,)),
            dma((N,)),
        ],
        compiler_params=pltpu.CompilerParams(
            collective_id=0, has_side_effects=True, vmem_limit_bytes=32 * 1024 * 1024
        ),
    )(
        wavenumber, sub_points, sub_currents, main_points, main_weight.reshape(1, -1),
        panel_ids.reshape(1, -1), panel_shift.reshape(1, -1), theta.reshape(1, -1), phi.reshape(1, -1),
    )


def solution(mesh):
    placed = (
        P(None, "src"),
        P("pol", "src", None),
        P(None, ("src", "tgt")),
        P(("src", "tgt")),
        P(("src", "tgt")),
        P(),
        P(),
        P(),
        P("freq"),
    )
    return jax.shard_map(
        functools.partial(on_device, mesh.shape["src"], mesh.shape["tgt"]),
        mesh=mesh,
        in_specs=placed,
        out_specs=(P("pol", ("src", "tgt"), "freq"), P("pol", ("src", "tgt"), "freq")),
        check_vma=False,
    )
```

```python
import functools
import math

import jax
import jax.numpy as jnp
from jax import lax
from jax.experimental import pallas as pl
from jax.experimental.pallas import tpu as pltpu
from jax.sharding import PartitionSpec as P

MESH = pl.DeviceIdType.MESH
VMEM_MIB = 56
TURN = 2.0 * math.pi
COS_HALF = (1.4142135381698608, -6.978850841522217, 5.739460468292236, -1.8835580348968506, 0.3106880187988281)
SIN_HALF = (4.442879676818848, -7.307816505432129, 3.5977745056152344, -0.7911993861198425)


def poly(coefs, s):
    value = coefs[-1]
    for coef in coefs[-2::-1]:
        value = value * s + coef
    return value


def turn_cos_sin(t):
    f = t - jnp.round(t)
    s = f * f
    half_cos = poly(COS_HALF, s)
    half_sin = f * poly(SIN_HALF, s)
    return 1.0 - half_sin * half_sin, half_cos * half_sin


def each(count, body, start=0):
    if count <= 16:
        for i in range(start, count):
            body(i)
    else:
        lax.fori_loop(start, count, lambda i, c: (body(i), c)[1], 0)


def thirds(x):
    first = x.astype(jnp.bfloat16).astype(jnp.float32)
    rest = x - first
    second = rest.astype(jnp.bfloat16).astype(jnp.float32)
    return first, second, rest - second


def left_rows(x):
    a, b, c = thirds(x)
    return jnp.concatenate([a, a, b, b, a, c], 0)


def right_rows(x):
    a, b, c = thirds(x)
    return jnp.concatenate([a, b, a, b, c, a], 0).astype(jnp.bfloat16)


def stack_rows(rows):
    n = rows[0].shape[1]
    index = lax.broadcasted_iota(jnp.int32, (8, n), 0)
    out = jnp.zeros((8, n), jnp.float32)
    for i, row in enumerate(rows):
        out = jnp.where(index == i, row, out)
    return out


def columns(rows):
    return jnp.transpose(stack_rows(rows))


def left_side(x):
    return jnp.transpose(left_rows(x)).astype(jnp.bfloat16)


def swapped(x):
    return pltpu.roll(x, x.shape[1] // 2, 1)


def paired(value, step, count):
    bit = 1
    while bit < count:
        value = value + bit * (step // bit % 2) * (1 - 2 * (value // bit % 2))
        bit *= 2
    return value


def kernel(
    S, T, sub_total, main_total,
    wave, sub_pts, sub_cur, main_pts, weight, ids, shift, theta, phi,
    cur_out, far_out,
    v_sub, v_cur, v_main, v_weight, v_ids, v_shift, v_theta, v_phi,
    pack, r2, kern, fkern, current, own, part, part_in, rad_sum, rad_own, rad_out, rad_in, turn_cols, cur_cols,
    in_sem, x_send, x_recv, a_send, a_recv, b_send, b_recv, c_send, c_recv,
):
    rows = main_pts.shape[1]
    half = rows // 2
    dirs = theta.shape[1]
    cols = sub_cur.shape[2]
    src, tgt, pol = lax.axis_index("src"), lax.axis_index("tgt"), lax.axis_index("pol")
    N = S * T * 2
    own_rows = dirs // (S * T)
    flat = (src * T + tgt) * 2 + pol
    bf16, f32 = jnp.bfloat16, jnp.float32

    def member(d):
        other = paired(flat, d, N)
        return other, {"src": other // (T * 2), "tgt": other // 2 % T, "pol": other % 2}

    loads = [
        pltpu.make_async_copy(a, b, in_sem.at[i])
        for i, (a, b) in enumerate([
            (main_pts, v_main), (weight, v_weight), (ids, v_ids), (shift, v_shift),
            (sub_cur.at[0], v_cur.at[pol]), (sub_pts, v_sub), (theta, v_theta), (phi, v_phi),
        ])
    ]
    for load in loads:
        load.start()
    barrier = pltpu.get_barrier_semaphore()

    def greet(d):
        pl.semaphore_signal(barrier, inc=1, device_id=member(d)[1], device_id_type=MESH)

    each(S, lambda i: greet(i * (2 * T)), 1)
    each(S, lambda i: each(2 * T, lambda j: greet(i * (2 * T) + j), 1))

    for load in loads[:4]:
        load.wait()
    q = wave[0] * (1.0 / TURN)
    sign = jnp.where(lax.broadcasted_iota(jnp.int32, (1, cols), 1) < cols // 2, 1.0, -1.0)
    lower = pol == 0

    def own_half(row):
        return jnp.where(lower, row[:, :half], row[:, half:])

    panels = shift.shape[1]
    panel = lax.broadcasted_iota(jnp.int32, (panels, rows), 0)
    shift_col = jnp.transpose(stack_rows([v_shift[...]]))[:, 0:1]
    chosen = jnp.sum(jnp.where(v_ids[...] == panel, shift_col, 0.0), 0, keepdims=True)
    cos_a, sin_a = turn_cos_sin(2.0 * q * chosen)
    factor = (1.0 / math.sqrt(sub_total)) * v_weight[...]
    fact_cos, fact_sin = factor * cos_a, factor * sin_a
    x, y, z = (v_main[i : i + 1, :] * q for i in range(3))
    pack[0] = stack_rows([
        own_half(row)
        for row in (-2.0 * x, -2.0 * y, -2.0 * z, x * x + y * y + z * z, jnp.ones_like(x), fact_cos, fact_sin)
    ])
    loads[4].wait()
    pl.semaphore_wait(barrier, N - 1)

    def points_copy(d):
        return pltpu.make_async_remote_copy(
            pack.at[0], pack.at[d], a_send.at[d], a_recv.at[d],
            device_id={"src": paired(src, d, S)}, device_id_type=MESH,
        )

    each(S, lambda d: points_copy(d).start(), 1)
    exchange = pltpu.make_async_remote_copy(
        v_cur.at[pol], v_cur.at[pol], x_send.at[0], x_recv.at[0],
        device_id={"pol": 1 - pol}, device_id_type=MESH,
    )
    exchange.start()
    for load in loads[5:]:
        load.wait()

    sx, sy, sz = (v_sub[i : i + 1, :] * q for i in range(3))
    sub_side = right_rows(
        stack_rows([sx, sy, sz, jnp.ones_like(sx), sx * sx + sy * sy + sz * sz])
    )
    cos_t, sin_t = turn_cos_sin(v_theta[...] * (1.0 / TURN))
    cos_p, sin_p = turn_cos_sin(v_phi[...] * (1.0 / TURN))
    phi_cols = columns([cos_p, sin_p])
    far_scale = 1.0 / math.sqrt(main_total)
    turn_cols[0] = jnp.broadcast_to(phi_cols[:, 0:1] * far_scale, (dirs, cols))
    turn_cols[1] = jnp.broadcast_to(phi_cols[:, 1:2] * far_scale, (dirs, cols))
    unit_side = left_side(stack_rows([-0.5 * sin_t * cos_p, -0.5 * sin_t * sin_p, -0.5 * cos_t]))
    fact_cols = columns([fact_cos, fact_sin])
    cur_cols[0] = jnp.broadcast_to(fact_cols[:, 0:1], (rows, cols))
    cur_cols[1] = fact_cols[:, 1:2] * sign
    step = 128

    def far_kernels(j):
        turns = jnp.dot(
            unit_side,
            right_rows(jnp.concatenate([pack[2 * j], pack[2 * j + 1]], 1)),
            preferred_element_type=f32,
        )
        for at in range(0, dirs, step):
            cosine, sine = turn_cos_sin(turns[at : at + step])
            fkern[j, at : at + step, :] = cosine.astype(bf16)
            fkern[j, dirs + at : dirs + at + step, :] = sine.astype(bf16)

    def part_copy(d, k):
        to = pol if k == 0 else 1 - pol
        return pltpu.make_async_remote_copy(
            part.at[d, to], part_in.at[2 * d + k], b_send.at[2 * d + k], b_recv.at[2 * d + k],
            device_id={"src": paired(src, d, S), "pol": to}, device_id_type=MESH,
        )

    def near_block(slots):
        packed = [pack[d] for d in slots]
        packed = packed[0] if len(packed) == 1 else jnp.concatenate(packed, 1)
        count = half * len(slots)
        turned = jnp.transpose(jnp.concatenate([left_rows(packed), packed], 0))
        r2[:count] = jnp.dot(turned[:, :48].astype(bf16), sub_side, preferred_element_type=f32)
        size = 16
        for at in range(0, count, size):
            square = r2[at : at + size, :]
            inverse = lax.rsqrt(square)
            cosine, sine = turn_cos_sin(square * inverse)
            inverse = inverse * (4.0 * q)
            kern[at : at + size, :] = (cosine * inverse).astype(bf16)
            kern[count + at : count + at + size, :] = (sine * inverse).astype(bf16)
        if len(slots) == 1 and slots[0] == 0:
            exchange.wait_recv()
        both = jnp.dot(
            kern[: 2 * count], jnp.concatenate([v_cur[0], v_cur[1]], 1), preferred_element_type=f32
        )
        fields, currents = [], []
        for c in (0, cols):
            field = both[:count, c : c + cols] + sign * swapped(both[count:, c : c + cols])
            fields.append(field)
            currents.append(
                (field * turned[:, 53:54] + swapped(field) * (turned[:, 54:55] * sign)).astype(bf16)
            )
        for i, d in enumerate(slots):
            at = slice(i * half, (i + 1) * half)
            for c in (0, 1):
                part[d, c] = fields[c][at].astype(bf16)
                current[d, :, c * cols : (c + 1) * cols] = currents[c][at]
            if isinstance(d, int) and d == 0:
                own[0], own[1] = fields[0], fields[1]
            else:
                part_copy(d, 0).start()
            part_copy(d, 1).start()

    def far_product(j):
        return jnp.dot(
            fkern[j],
            jnp.concatenate([current[2 * j], current[2 * j + 1]], 0),
            preferred_element_type=f32,
        )

    near_block((0,))
    if S <= 16:
        for j in range(1, S // 2):
            points_copy(2 * j).wait_recv()
            points_copy(2 * j + 1).wait_recv()
            near_block((2 * j, 2 * j + 1))
            far_kernels(j)
    else:

        def pair_step(j, c):
            points_copy(2 * j).wait_recv()
            points_copy(2 * j + 1).wait_recv()
            near_block((2 * j, 2 * j + 1))
            far_kernels(j)
            return c

        lax.fori_loop(1, S // 2, pair_step, 0)
    points_copy(1).wait_recv()
    near_block((1,))
    far_kernels(0)
    rad_sum[...] = far_product(0)

    def add_pair(j):
        rad_sum[...] += far_product(j)

    each(S // 2, add_pair, 1)
    for at in range(0, dirs, step):
        real = rad_sum[at : at + step]
        imag = rad_sum[dirs + at : dirs + at + step]
        first, second = (
            real[:, c : c + cols] - sign * swapped(imag[:, c : c + cols]) for c in (0, cols)
        )
        cosine, sine = turn_cols[0, at : at + step], turn_cols[1, at : at + step]
        co_polar = cosine * first + sine * second
        cross_polar = cosine * second - sine * first
        rad_own[0, at : at + step] = co_polar
        rad_own[1, at : at + step] = cross_polar
        rad_out[0, at : at + step] = co_polar.astype(bf16)
        rad_out[1, at : at + step] = cross_polar.astype(bf16)

    def far_copy(d):
        other, where = member(d)
        first = pl.multiple_of(other // 2 * own_rows, own_rows)
        return pltpu.make_async_remote_copy(
            rad_out.at[other % 2, pl.ds(first, own_rows)], rad_in.at[d], c_send.at[d], c_recv.at[d],
            device_id=where, device_id_type=MESH,
        )

    each(N, lambda i: far_copy(N - i).start(), 1)

    exchange.wait_send()
    each(S, lambda d: points_copy(d).wait_send(), 1)
    part_copy(0, 1).wait_send()
    each(S, lambda d: (part_copy(d, 0).wait_send(), part_copy(d, 1).wait_send()), 1)
    for k in (0, 1):
        if k == 0:
            induced = own[pol]
        else:
            part_copy(0, 1).wait_recv()
            induced = part_in[1].astype(f32)

        def added(d, total):
            part_copy(d, k).wait_recv()
            return total + part_in[2 * d + k].astype(f32)

        if S <= 16:
            for d in range(1, S):
                induced = added(d, induced)
        else:
            induced = lax.fori_loop(1, S, added, induced)
        there = pl.ds(pl.multiple_of((pol if k == 0 else 1 - pol) * half, half), half)
        cur_out[0, there] = (
            induced * cur_cols[0, there] + swapped(induced) * cur_cols[1, there]
        ).astype(bf16)

    each(N, lambda d: far_copy(d).wait(), 1)
    here = pl.ds(pl.multiple_of((src * T + tgt) * own_rows, own_rows), own_rows)
    total = rad_own[pol, here]
    if N <= 16:
        for d in range(1, N):
            total = total + rad_in[d].astype(f32)
    else:
        total = lax.fori_loop(1, N, lambda d, t: t + rad_in[d].astype(f32), total)
    far_out[0] = total


def on_device(S, T, sub_points, sub_currents, main_points, main_weight, panel_ids, panel_shift, theta, phi, wavenumber):
    rows, subs = main_points.shape[1], sub_points.shape[1]
    half = rows // 2
    cols = sub_currents.shape[2]
    dirs = theta.shape[0]
    panels = panel_shift.shape[0]
    N = S * T * 2
    own_rows = dirs // (S * T)
    f32, bf16 = jnp.float32, jnp.bfloat16
    hbm = pl.BlockSpec(memory_space=pl.ANY)
    vmem = pl.BlockSpec(memory_space=pltpu.VMEM)
    dma = pltpu.SemaphoreType.DMA
    return pl.pallas_call(
        functools.partial(kernel, S, T, subs * S, rows * S * T),
        out_shape=(
            jax.ShapeDtypeStruct((1, rows, cols), bf16),
            jax.ShapeDtypeStruct((1, own_rows, cols), f32),
        ),
        in_specs=[pl.BlockSpec(memory_space=pltpu.SMEM)] + [hbm] * 8,
        out_specs=(vmem, vmem),
        scratch_shapes=[
            pltpu.VMEM((3, subs), f32),
            pltpu.VMEM((2, subs, cols), bf16),
            pltpu.VMEM((3, rows), f32),
            pltpu.VMEM((1, rows), f32),
            pltpu.VMEM((1, rows), jnp.int32),
            pltpu.VMEM((1, panels), f32),
            pltpu.VMEM((1, dirs), f32),
            pltpu.VMEM((1, dirs), f32),
            pltpu.VMEM((S, 8, half), f32),
            pltpu.VMEM((rows, subs), f32),
            pltpu.VMEM((2 * rows, subs), bf16),
            pltpu.VMEM((S // 2, 2 * dirs, rows), bf16),
            pltpu.VMEM((S, half, 2 * cols), bf16),
            pltpu.VMEM((2, half, cols), f32),
            pltpu.VMEM((S, 2, half, cols), bf16),
            pltpu.VMEM((2 * S, half, cols), bf16),
            pltpu.VMEM((2 * dirs, 2 * cols), f32),
            pltpu.VMEM((2, dirs, cols), f32),
            pltpu.VMEM((2, dirs, cols), bf16),
            pltpu.VMEM((N, own_rows, cols), bf16),
            pltpu.VMEM((2, dirs, cols), f32),
            pltpu.VMEM((2, rows, cols), f32),
            dma((8,)),
            dma((1,)),
            dma((1,)),
            dma((S,)),
            dma((S,)),
            dma((2 * S,)),
            dma((2 * S,)),
            dma((N,)),
            dma((N,)),
        ],
        compiler_params=pltpu.CompilerParams(
            collective_id=0, has_side_effects=True, vmem_limit_bytes=VMEM_MIB * 1024 * 1024
        ),
    )(
        wavenumber, sub_points, sub_currents, main_points, main_weight.reshape(1, -1),
        panel_ids.reshape(1, -1), panel_shift.reshape(1, -1), theta.reshape(1, -1), phi.reshape(1, -1),
    )


def solution(mesh):
    placed = (
        P(None, "src"),
        P("pol", "src", None),
        P(None, ("src", "tgt")),
        P(("src", "tgt")),
        P(("src", "tgt")),
        P(),
        P(),
        P(),
        P("freq"),
    )
    return jax.shard_map(
        functools.partial(on_device, mesh.shape["src"], mesh.shape["tgt"]),
        mesh=mesh,
        in_specs=placed,
        out_specs=(P("pol", ("src", "tgt"), "freq"), P("pol", ("src", "tgt"), "freq")),
        check_vma=False,
    )
```
